32 devices in a mesh: tm: 16 (over z, x, core), head: 2 (over y).
Axes of the slice: x: 2, y: 2, z: 4, core: 2. Of those that a mesh axis runs over, the one named last changes fastest.
Arguments:
- frames: bfloat16 [16, 512, 1152], P('tm', None, 'head'), may hold values from -6 to 6
- modulation: float32 [3, 1152], replicated, may hold values from -4 to 4
- w_qkv: bfloat16 [3, 1152, 1152], P(None, None, 'head'), may hold values from -1 to 1
- w_out: bfloat16 [1152, 1152], P('head'), may hold values from -0.375 to 0.375
- conv_taps: float32 [3, 1152], P(None, 'head'), may hold values from -3 to 3
- anchors: int32 [1], replicated, may hold values from 0 to 15
Outputs:
- block_out: bfloat16 [16, 512, 1152], P('tm', None, 'head')
The draws below stay inside these ranges and needn't reach their ends.
All inputs are finite; a program needn't handle non-finite values.
Results may differ from the reference program's by a relative error of at most 0.011.
Values may be sent and summed in bfloat16 or wider, within the bound.
No kernel may reach another device: no remote copies, remote signals or barrier semaphores. Data moves between devices by JAX's collectives and lax.ppermute only.
A program may use at most 64 MiB of HBM per device.

```python
import jax
import jax.numpy as jnp
from jax import lax

D = 1152
HEADS = 16
HS = 72
P_SIZE = 512
SEG = 16
FRAMES = 16
SEGMENTS = 1


def draw_w_qkv(key, part):
    key_query, key_key, key_value = jax.random.split(key, 3)
    fan_scale = D ** (-0.5)
    w_query = jax.random.normal(key_query, (D, D), jnp.float32) * (1.5 * fan_scale)
    w_key = jax.random.normal(key_key, (D, D), jnp.float32) * (1.5 * fan_scale)
    w_value = jax.random.normal(key_value, (D, D), jnp.float32) * fan_scale
    stacked = jnp.stack([w_query, w_key, w_value])
    return jnp.clip(stacked, -1.0, 1.0).astype(jnp.bfloat16)


def block_levels(stream_key, dims, pieces, low, top_value):
    def one(position, blocks):
        heights = jax.random.uniform(jax.random.fold_in(jax.random.fold_in(stream_key, 6), position), (blocks,), jnp.float32, low / len(pieces), top_value / len(pieces))
        return jnp.repeat(jnp.exp(heights), dims[position] // blocks).reshape((-1,) + (1,) * (len(dims) - position - 1))

    level = one(*pieces[0])
    for cut in pieces[1:]:
        level = level * one(*cut)
    return level


def noise(stream_key, shape, deviation, limit, shards=(), kind=jnp.bfloat16):
    entries = jax.random.normal(stream_key, shape, jnp.float32) * deviation
    if len(shards) > 0:
        entries = block_levels(stream_key, shape, shards, -0.22, 0.18) * entries
    return jnp.clip(entries, min=-limit, max=limit).astype(kind)


def setup_inputs(seed: int = 0) -> dict:
    arg_keys = jax.random.split(jax.random.key(seed), 7)
    return {
        "frames": noise(arg_keys[0], (FRAMES, P_SIZE, D), 1.0, 6.0, ((0, 16), (2, 2))),
        "modulation": noise(arg_keys[1], (3, D), 0.8, 4.0, (), jnp.float32),
        "w_qkv": draw_w_qkv(jax.random.fold_in(arg_keys[6], 71), 0),
        "w_out": noise(arg_keys[3], (D, D), (D // 4) ** -0.5, 0.375, ((0, 2),)),
        "conv_taps": noise(arg_keys[4], (3, D), 0.5, 3.0, ((1, 2),), jnp.float32),
        "anchors": jax.random.randint(arg_keys[5], (SEGMENTS,), 0, SEG).astype(jnp.int32),
    }


EPSILON = 1e-06

def modulate(frame_rows, modulation):
    values = frame_rows.astype(jnp.float32)
    average = lax.optimization_barrier(jnp.mean(values, axis=-1, keepdims=True))
    centred = values - average
    variance = lax.optimization_barrier(jnp.mean(centred * centred, axis=-1, keepdims=True))
    normed = centred * lax.rsqrt(variance + EPSILON)
    return (normed * (1.0 + modulation[1]) + modulation[0]).astype(jnp.bfloat16)

def project_all(frame_rows, modulation, w_qkv):
    normed = modulate(frame_rows, modulation)
    return jnp.einsum('pd,cde->cpe', normed.astype(jnp.float32), w_qkv.astype(jnp.float32)).astype(jnp.bfloat16)

def attend(queries, key_rows, value_rows):
    scores = jnp.einsum('qhs,khs->hqk', queries.astype(jnp.float32), key_rows.astype(jnp.float32)) * HS ** (-0.5)
    row_max = lax.optimization_barrier(jnp.max(scores, axis=-1, keepdims=True))
    weights = jnp.exp(scores - row_max)
    weights = (weights / lax.optimization_barrier(jnp.sum(weights, axis=-1, keepdims=True))).astype(jnp.bfloat16)
    return jnp.einsum('hqk,khs->qhs', weights.astype(jnp.float32), value_rows.astype(jnp.float32)).astype(jnp.bfloat16)

def reference(frames, modulation, w_qkv, w_out, conv_taps, anchors):
    frame_count, tokens, width = frames.shape
    anchor_rows = (jnp.arange(SEGMENTS, dtype=jnp.int32) * SEG + anchors).astype(jnp.int32)

    def anchor_data(row):
        frame_rows = lax.dynamic_index_in_dim(frames, row, 0, keepdims=False)
        return project_all(frame_rows, modulation, w_qkv)[1:]
    anchor_pairs = lax.map(anchor_data, anchor_rows)

    def one_frame(frame_index):
        frame_rows = lax.dynamic_index_in_dim(frames, frame_index, 0, keepdims=False)
        triple = project_all(frame_rows, modulation, w_qkv)
        anchor_kv = lax.dynamic_index_in_dim(anchor_pairs, frame_index // SEG, 0, keepdims=False)
        key_rows = jnp.concatenate([triple[1], anchor_kv[0]], axis=0).reshape(2 * tokens, HEADS, HS)
        value_rows = jnp.concatenate([triple[2], anchor_kv[1]], axis=0).reshape(2 * tokens, HEADS, HS)
        attended = attend(triple[0].reshape(tokens, HEADS, HS), key_rows, value_rows).reshape(tokens, width)
        projected = jnp.dot(attended, w_out, preferred_element_type=jnp.float32)
        return (frame_rows.astype(jnp.float32) + modulation[2] * projected).astype(jnp.bfloat16)
    hidden = lax.map(one_frame, jnp.arange(frame_count, dtype=jnp.int32))
    padded = jnp.pad(hidden, ((1, 1), (0, 0), (0, 0))).astype(jnp.float32)
    block_out = padded[1:-1] + conv_taps[0] * padded[:-2] + conv_taps[1] * padded[1:-1] + conv_taps[2] * padded[2:]
    return block_out.astype(jnp.bfloat16)
```

```python
import functools

import jax
import jax.numpy as jnp
from jax import lax
from jax.experimental import pallas as pl
from jax.experimental.pallas import tpu as pltpu
from jax.sharding import PartitionSpec as P

HS = 72
SEG = 16
LANES = 128
EPSILON = 1e-06
LOG2_E = 1.4426950408889634

IN_CHUNKS = 2
OUT_CHUNKS = 4


def exchanged(block, bit):
    count = lax.axis_size("tm")
    return lax.ppermute(block, "tm", [(i, i ^ bit) for i in range(count)])


def shifted(block, bit, shift):
    frames, heads = lax.axis_size("tm"), lax.axis_size("head")
    route = [
        (f * heads + h, (f ^ bit) * heads + (h + shift) % heads)
        for f in range(frames)
        for h in range(heads)
    ]
    return lax.ppermute(block, ("tm", "head"), route)


def project_kernel(blocks, parts, scales, order_ref, *refs):
    pieces = refs[: blocks * parts]
    modulation_ref, w_ref = refs[blocks * parts : blocks * parts + 2]
    outs = refs[blocks * parts + 2 :]
    first = w_ref.shape[0] - len(outs)
    order = [order_ref[j] for j in range(parts)]
    start = 0
    for block in range(blocks):
        values = [ref[...].astype(jnp.float32) for ref in pieces[block * parts : (block + 1) * parts]]
        rows = values[0].shape[0]
        features = sum(v.shape[1] for v in values)
        average = sum(jnp.sum(v, axis=1, keepdims=True) for v in values) / features
        centred = [v - average for v in values]
        variance = sum(jnp.sum(c * c, axis=1, keepdims=True) for c in centred) / features
        scale = lax.rsqrt(variance + EPSILON)
        normed = [
            (c * scale * (1.0 + modulation_ref[1, k]) + modulation_ref[0, k]).astype(jnp.bfloat16)
            for c, k in zip(centred, order)
        ]
        for index, (out, factor) in enumerate(zip(outs, scales)):
            total = sum(
                jnp.dot(n, w_ref[first + index, k], preferred_element_type=jnp.float32)
                for n, k in zip(normed, order)
            )
            is_value = index == len(outs) - 1
            if factor is not None:
                total = total * factor
            total = total.astype(jnp.bfloat16)
            lane = lax.broadcasted_iota(jnp.int32, (rows, LANES), 1)
            filler = jnp.where(lane == HS, 1.0 if is_value else 0.0, 0.0).astype(jnp.bfloat16)
            for head in range(out.shape[0]):
                out[head, pl.ds(start, rows), :] = filler
                out[head, pl.ds(start, rows), 0:HS] = total[:, head * HS : (head + 1) * HS]
        start += rows


def project(blocks, order, modulation, w_qkv, with_queries):
    parts = len(blocks[0])
    tokens = sum(block[0].shape[0] for block in blocks)
    heads = w_qkv.shape[-1] // HS
    count = 3 if with_queries else 2
    scales = [HS ** (-0.5) * LOG2_E, None, None][3 - count :]
    out = jax.ShapeDtypeStruct((heads, tokens, LANES), jnp.bfloat16)
    vmem = pl.BlockSpec(memory_space=pltpu.VMEM)
    flat = [piece for block in blocks for piece in block]
    width = w_qkv.shape[1] * w_qkv.shape[2]
    return pl.pallas_call(
        functools.partial(project_kernel, len(blocks), parts, scales),
        out_shape=[out] * count,
        in_specs=[pl.BlockSpec(memory_space=pltpu.SMEM)] + [vmem] * (len(flat) + 2),
        out_specs=[vmem] * count,
        compiler_params=pltpu.CompilerParams(vmem_limit_bytes=40 * 2**20),
        cost_estimate=pl.CostEstimate(
            flops=2 * tokens * width * w_qkv.shape[-1] * count,
            bytes_accessed=count * (w_qkv.size // 3 + tokens * heads * LANES) * 2,
            transcendentals=0,
        ),
    )(order, *flat, modulation, w_qkv)


def attend_kernel(
    parts, head_ref, q_ref, ko_ref, vo_ref, ka_ref, va_ref, w_ref, own_ref, send_ref, attended
):
    heads = q_ref.shape[0]
    contract = (((1,), (1,)), ((), ()))
    for head in range(heads):
        queries = q_ref[head]
        own = lax.dot_general(queries, ko_ref[head], contract, preferred_element_type=jnp.float32)
        anchor = lax.dot_general(queries, ka_ref[head], contract, preferred_element_type=jnp.float32)
        top = jnp.maximum(
            jnp.max(own, axis=1, keepdims=True), jnp.max(anchor, axis=1, keepdims=True)
        )
        own = jnp.exp2(own - top).astype(jnp.bfloat16)
        anchor = jnp.exp2(anchor - top).astype(jnp.bfloat16)
        total = jnp.dot(own, vo_ref[head], preferred_element_type=jnp.float32)
        total += jnp.dot(anchor, va_ref[head], preferred_element_type=jnp.float32)
        result = total[:, :HS] / total[:, HS : HS + 1]
        attended[:, head * HS : (head + 1) * HS] = result.astype(jnp.bfloat16)
    terms = jnp.dot(attended[...], w_ref[...], preferred_element_type=jnp.float32)
    width = own_ref.shape[1]
    me = head_ref[0]
    for part in range(parts):
        columns = terms[:, part * width : (part + 1) * width]
        step = lax.rem(part - me + parts, parts)

        @pl.when(step == 0)
        def _():
            own_ref[...] = columns

        @pl.when(step != 0)
        def _():
            send_ref[lax.max(step - 1, 0)] = columns.astype(jnp.bfloat16)


def attend(me, parts, queries, own_kv, anchor_kv, w_out, chunk, chunks):
    heads, tokens, _ = queries.shape
    rows = tokens // chunks
    width = w_out.shape[1] // parts
    vmem = pl.BlockSpec(memory_space=pltpu.VMEM)

    def whole(x):
        return pl.BlockSpec(x.shape, lambda i: (0,) * x.ndim)

    keys = 2 * tokens
    return pl.pallas_call(
        functools.partial(attend_kernel, parts),
        grid=(1,),
        out_shape=[
            jax.ShapeDtypeStruct((rows, width), jnp.float32),
            jax.ShapeDtypeStruct((parts - 1, rows, width), jnp.bfloat16),
        ],
        in_specs=[
            pl.BlockSpec(memory_space=pltpu.SMEM),
            pl.BlockSpec((heads, rows, LANES), lambda i: (0, chunk, 0)),
        ]
        + [whole(x) for x in (*own_kv, *anchor_kv, w_out)],
        out_specs=[
            pl.BlockSpec((rows, width), lambda i: (0, 0)),
            pl.BlockSpec((parts - 1, rows, width), lambda i: (0, 0, 0)),
        ],
        scratch_shapes=[pltpu.VMEM((rows, heads * HS), jnp.bfloat16)],
        compiler_params=pltpu.CompilerParams(vmem_limit_bytes=40 * 2**20),
        cost_estimate=pl.CostEstimate(
            flops=4 * heads * rows * keys * LANES + 2 * rows * w_out.size,
            bytes_accessed=8 * heads * tokens * LANES + 2 * w_out.size,
            transcendentals=heads * rows * keys,
        ),
    )(me, queries, *own_kv, *anchor_kv, w_out)


def anchor_rows(frame, anchor):
    tokens = frame.shape[0]
    heads = lax.axis_size("head")
    index = lax.axis_index("tm") % SEG
    half, quarter = tokens // 2, tokens // 4

    def bit(value, number):
        return (value >> number) & 1

    def same(number):
        return bit(index, number) == bit(anchor, number)

    core, side = bit(index, 0), bit(index, 1)
    kept = lax.dynamic_slice_in_dim(frame, core * half, half, 0)
    sent = lax.dynamic_slice_in_dim(frame, (1 - core) * half, half, 0)
    block = jnp.where(same(0), kept, exchanged(sent, 1))
    kept = lax.dynamic_slice_in_dim(block, side * quarter, quarter, 0)
    sent = lax.dynamic_slice_in_dim(block, (1 - side) * quarter, quarter, 0)
    block = jnp.where(same(1), kept, exchanged(sent, 2))
    for number in range(2, SEG.bit_length() - 1):
        block = jnp.where(same(number), block, exchanged(block, 1 << number))
    rows = []
    for across in (0, 2):
        rows.append(
            [block if across == 0 and step == 0 else shifted(block, across, step) for step in range(heads)]
        )
    return rows + [[exchanged(piece, 1) for piece in row] for row in rows]


def local(frames, modulation, w_qkv, w_out, conv_taps, anchors):
    frame = frames[0]
    tokens, width = frame.shape
    parts = lax.axis_size("head")
    place, me = lax.axis_index("tm"), lax.axis_index("head")
    anchor = lax.dynamic_index_in_dim(anchors, place // SEG, 0, keepdims=False)
    order = ((me - jnp.arange(parts)) % parts).astype(jnp.int32)
    me_ref = me.astype(jnp.int32).reshape(1)
    by_part = modulation.reshape(3, parts, width)
    w_parts = w_qkv.reshape(3, parts, width, width)

    rows = tokens // IN_CHUNKS
    own_rows = []
    for chunk in range(IN_CHUNKS):
        piece = frame[chunk * rows : (chunk + 1) * rows]
        own_rows.append([piece] + [shifted(piece, 0, step) for step in range(1, parts)])
    far_rows = anchor_rows(frame, anchor)
    queries, *own_kv = project(own_rows, order, by_part, w_parts, True)
    anchor_kv = project(far_rows, order, by_part, w_parts, False)

    gate = lax.dynamic_index_in_dim(by_part[2], me, 0, keepdims=False)
    rows = tokens // OUT_CHUNKS
    count = lax.axis_size("tm")
    odd = [(i, i + 1) for i in range(1, count - 1, 2)]
    odd = odd + [(j, i) for i, j in odd]
    outs = []
    is_even = place % 2 == 0
    tap_near = jnp.where(is_even, conv_taps[2], conv_taps[0])
    tap_far = jnp.where(is_even, conv_taps[0], conv_taps[2])
    for chunk in range(OUT_CHUNKS):
        total, send = attend(me_ref, parts, queries, own_kv, anchor_kv, w_out, chunk, OUT_CHUNKS)
        for step in range(1, parts):
            total = total + shifted(send[step - 1], 0, step).astype(jnp.float32)
        piece = frame[chunk * rows : (chunk + 1) * rows].astype(jnp.float32)
        hidden = (piece + gate * total).astype(jnp.bfloat16)
        near = exchanged(hidden, 1).astype(jnp.float32)
        far = lax.ppermute(hidden, "tm", odd).astype(jnp.float32)
        hidden = hidden.astype(jnp.float32)
        out = hidden + conv_taps[1] * hidden + tap_near * near + tap_far * far
        outs.append(out.astype(jnp.bfloat16))
    return jnp.concatenate(outs, axis=0)[None]


def solution(mesh):
    in_specs = (
        P("tm", None, "head"),
        P(),
        P(None, None, "head"),
        P("head", None),
        P(None, "head"),
        P(),
    )
    out_specs = P("tm", None, "head")
    return jax.shard_map(local, mesh=mesh, in_specs=in_specs, out_specs=out_specs, check_vma=False)
```

```python
import functools

import jax
import jax.numpy as jnp
from jax import lax
from jax.experimental import pallas as pl
from jax.experimental.pallas import tpu as pltpu
from jax.sharding import PartitionSpec as P

HS = 72
SEG = 16
LANES = 128
VALUE_ROWS = 80
EPSILON = 1e-06
LOG2_E = 1.4426950408889634

OUT_CHUNKS = 2
IN_CHUNKS = 1
CONV_FLOPS = 10**10
VMEM_BYTES = 32 * 2**20
VMEM = pl.BlockSpec(memory_space=pltpu.VMEM)
SMEM = pl.BlockSpec(memory_space=pltpu.SMEM)
HBM = pl.BlockSpec(memory_space=pltpu.HBM)


def outside(x):
    return pltpu.with_memory_space_constraint(x, pltpu.HBM)


def exchanged(block, bit):
    count = lax.axis_size("tm")
    return lax.ppermute(block, "tm", [(i, i ^ bit) for i in range(count)])


def shifted(block, bit, shift):
    frames, heads = lax.axis_size("tm"), lax.axis_size("head")
    route = [
        (f * heads + h, (f ^ bit) * heads + (h + shift) % heads)
        for f in range(frames)
        for h in range(heads)
    ]
    return lax.ppermute(block, ("tm", "head"), route)


def project_kernel(blocks, parts, factor, order_ref, modulation_ref, w_hbm, *refs):
    pieces = refs[: blocks * parts]
    *query_ref, key_ref, value_ref, x_ref, shift_ref, scale_ref, w_ref, w_sem = refs[blocks * parts :]
    features, tokens = x_ref.shape
    width = features // parts
    step = tokens // blocks
    heads = key_ref.shape[0]
    count = w_ref.shape[0]
    loads = [
        pltpu.make_async_copy(w_hbm.at[3 - count + c], w_ref.at[c], w_sem.at[c]) for c in range(count)
    ]
    for load in loads:
        load.start()
    for block in range(blocks):
        for part in range(parts):
            start = pl.multiple_of(order_ref[part] * width, 32)
            x_ref[pl.ds(start, width), block * step : (block + 1) * step] = pieces[
                block * parts + part
            ][...]
    columns = jnp.concatenate([modulation_ref[...], jnp.zeros((5, features), jnp.float32)]).T
    shift_ref[...] = jnp.broadcast_to(columns[:, 0:1], (features, LANES))
    scale_ref[...] = jnp.broadcast_to(1.0 + columns[:, 1:2], (features, LANES))
    for start in range(0, tokens, LANES):
        values = x_ref[:, start : start + LANES].astype(jnp.float32)
        centred = values - jnp.sum(values, axis=0, keepdims=True) / features
        variance = jnp.sum(centred * centred, axis=0, keepdims=True) / features
        normed = centred * lax.rsqrt(variance + EPSILON)
        x_ref[:, start : start + LANES] = (normed * scale_ref[...] + shift_ref[...]).astype(jnp.bfloat16)

    row = lax.broadcasted_iota(jnp.int32, (VALUE_ROWS - HS, tokens), 0)
    ones = jnp.where(row == 0, 1.0, 0.0).astype(jnp.bfloat16)
    group = 2
    for c in range(count):
        loads[c].wait()
        for first in range(0, heads, group):
            total = jnp.dot(
                w_ref[c, first * HS : (first + group) * HS],
                x_ref[...],
                preferred_element_type=jnp.float32,
            )
            for head in range(first, first + group):
                rows = total[(head - first) * HS : (head - first + 1) * HS]
                if c == count - 1:
                    value_ref[head, 0:HS, :] = rows.astype(jnp.bfloat16)
                    value_ref[head, HS:, :] = ones
                elif c == count - 2:
                    key_ref[head, :, 0:HS] = rows.T.astype(jnp.bfloat16)
                    key_ref[head, :, HS:] = jnp.zeros((tokens, LANES - HS), jnp.bfloat16)
                else:
                    query_ref[0][head, 0:HS, :] = (rows * factor).astype(jnp.bfloat16)
                    query_ref[0][head, HS:, :] = jnp.zeros((LANES - HS, tokens), jnp.bfloat16)


def project(blocks, order, modulation, w_qkv, with_queries):
    parts = len(blocks[0])
    tokens = sum(block[0].shape[1] for block in blocks)
    _, width, features = w_qkv.shape
    heads = width // HS
    count = 3 if with_queries else 2
    queries = jax.ShapeDtypeStruct((heads, LANES, tokens), jnp.bfloat16)
    keys = jax.ShapeDtypeStruct((heads, tokens, LANES), jnp.bfloat16)
    values = jax.ShapeDtypeStruct((heads, VALUE_ROWS, tokens), jnp.bfloat16)
    flat = [piece for block in blocks for piece in block]
    return pl.pallas_call(
        functools.partial(project_kernel, len(blocks), parts, HS ** (-0.5) * LOG2_E),
        out_shape=[queries, keys, values][3 - count :],
        in_specs=[SMEM, VMEM, HBM] + [VMEM] * len(flat),
        out_specs=[VMEM] * count,
        scratch_shapes=[
            pltpu.VMEM((features, tokens), jnp.bfloat16),
            pltpu.VMEM((features, LANES), jnp.float32),
            pltpu.VMEM((features, LANES), jnp.float32),
            pltpu.VMEM((count, width, features), jnp.bfloat16),
            pltpu.SemaphoreType.DMA((count,)),
        ],
        compiler_params=pltpu.CompilerParams(vmem_limit_bytes=VMEM_BYTES),
        cost_estimate=pl.CostEstimate(
            flops=2 * tokens * features * width * count,
            bytes_accessed=count * 2 * (features * width + tokens * heads * LANES),
            transcendentals=0,
        ),
    )(order, modulation, outside(w_qkv), *flat)


def attend_kernel(parts, start, me_ref, *refs):
    sources = refs[:8]
    own_ref, send_ref = refs[8:10]
    buffers = refs[10:18]
    attended, terms, scores, weights, sems = refs[18:]
    q_ref, *keys_values = buffers[:7]
    w_ref = buffers[7]
    keys, values = keys_values[0::2], keys_values[1::2]
    heads = q_ref.shape[0]
    width, rows = own_ref.shape
    firsts = (0, 1) if heads < 4 else (0, 1, 3)
    loads = []
    for first, last in zip(firsts, (*firsts[1:], heads)):
        span = pl.ds(first, last - first)
        loads.append([])
        for i, (source, buffer) in enumerate(zip(sources[:7], buffers[:7])):
            part = source.at[span]
            if i == 0:
                part = source.at[span, :, pl.ds(start, rows)]
            loads[-1].append(
                pltpu.make_async_copy(part, buffer.at[span], sems.at[first, i])
            )
    load_w = pltpu.make_async_copy(sources[7], w_ref, sems.at[0, 7])
    for group in loads:
        for load in group:
            load.start()
    load_w.start()
    spans, total = [], 0
    for ref in keys:
        spans.append((total, total + ref.shape[1]))
        total += ref.shape[1]

    def score(head):
        if head in firsts:
            for load in loads[firsts.index(head)]:
                load.wait()
        for ref, (low, high) in zip(keys, spans):
            scores[head % 2, low:high] = jnp.dot(
                ref[head], q_ref[head], preferred_element_type=jnp.float32
            )

    def weigh(head):
        values = scores[head % 2]
        top = jnp.max(values, axis=0, keepdims=True)
        weights[head % 2] = jnp.exp2(values - top).astype(jnp.bfloat16)

    def collect(head):
        total = sum(
            jnp.dot(ref[head], weights[head % 2, low:high], preferred_element_type=jnp.float32)
            for ref, (low, high) in zip(values, spans)
        )
        attended[head * HS : (head + 1) * HS, :] = total[:HS] / total[HS : HS + 1]

    for head in range(heads + 2):
        if head < heads:
            score(head)
        if head >= 2:
            collect(head - 2)
        if 1 <= head <= heads:
            weigh(head - 1)
    load_w.wait()
    terms[...] = jnp.dot(
        w_ref[...], attended[...].astype(jnp.bfloat16), preferred_element_type=jnp.float32
    )
    me = me_ref[0]
    own_ref[...] = terms[pl.ds(pl.multiple_of(me * width, 32), width), :]
    for step in range(1, parts):
        other = lax.rem(me + step, parts)
        send_ref[step - 1] = terms[pl.ds(pl.multiple_of(other * width, 32), width), :].astype(
            jnp.bfloat16
        )


def attend(me, parts, queries, kvs, w_out, start, rows):
    heads, _, tokens = queries.shape
    features, width = w_out.shape
    keys = 2 * tokens
    arrays = [queries, *kvs[0], *kvs[1], *kvs[2], w_out]
    buffers = [pltpu.VMEM((heads, LANES, rows), jnp.bfloat16)]
    buffers += [pltpu.VMEM(x.shape, x.dtype) for x in arrays[1:]]
    return pl.pallas_call(
        functools.partial(attend_kernel, parts, start),
        out_shape=[
            jax.ShapeDtypeStruct((features // parts, rows), jnp.float32),
            jax.ShapeDtypeStruct((parts - 1, features // parts, rows), jnp.bfloat16),
        ],
        in_specs=[SMEM] + [HBM] * 8,
        out_specs=[VMEM] * 2,
        scratch_shapes=buffers
        + [
            pltpu.VMEM((heads * HS, rows), jnp.float32),
            pltpu.VMEM((features, rows), jnp.float32),
            pltpu.VMEM((2, keys, rows), jnp.float32),
            pltpu.VMEM((2, keys, rows), jnp.bfloat16),
            pltpu.SemaphoreType.DMA((heads, 8)),
        ],
        compiler_params=pltpu.CompilerParams(vmem_limit_bytes=VMEM_BYTES),
        cost_estimate=pl.CostEstimate(
            flops=4 * heads * rows * keys * LANES + 2 * rows * w_out.size,
            bytes_accessed=8 * heads * tokens * LANES + 2 * w_out.size,
            transcendentals=heads * rows * keys,
        ),
    )(me, *[outside(x) for x in arrays])


def tied(x, *others):
    return lax.optimization_barrier((x, *others))[0]


def conv_kernel(start, hidden_ref, near_ref, far_ref, taps_ref, *refs):
    out_hbm, out_ref, sem = refs[-3:]
    width, rows = out_ref.shape
    hidden = hidden_ref[...].astype(jnp.float32)
    total = hidden + taps_ref[:, 1:2] * hidden
    total += taps_ref[:, 0:1] * near_ref[...].astype(jnp.float32)
    total += taps_ref[:, 2:3] * far_ref[...].astype(jnp.float32)
    out_ref[...] = total.astype(jnp.bfloat16)
    store = pltpu.make_async_copy(out_ref, out_hbm.at[:, start : start + rows], sem)
    store.start()
    store.wait()


def convolved(hidden, near, far, taps, start, tokens, out):
    width, rows = hidden.shape
    before = [] if out is None else [out]
    return pl.pallas_call(
        functools.partial(conv_kernel, start),
        out_shape=jax.ShapeDtypeStruct((width, tokens), jnp.bfloat16),
        in_specs=[VMEM] * 4 + [HBM] * len(before),
        out_specs=HBM,
        scratch_shapes=[pltpu.VMEM((width, rows), jnp.bfloat16), pltpu.SemaphoreType.DMA],
        input_output_aliases={4: 0} if before else {},
        compiler_params=pltpu.CompilerParams(vmem_limit_bytes=VMEM_BYTES),
        cost_estimate=pl.CostEstimate(flops=CONV_FLOPS, bytes_accessed=8 * width * rows, transcendentals=0),
    )(hidden, near, far, taps, *before)


def local(frames, modulation, w_qkv, w_out, conv_taps, anchors):
    frame = frames[0].T
    width, tokens = frame.shape
    parts, count = lax.axis_size("head"), lax.axis_size("tm")
    place, me = lax.axis_index("tm"), lax.axis_index("head")
    anchor = lax.dynamic_index_in_dim(anchors, place // SEG, 0, keepdims=False)
    order = ((me - jnp.arange(parts)) % parts).astype(jnp.int32)
    me_ref = me.astype(jnp.int32).reshape(1)
    w_qkv = jnp.swapaxes(w_qkv, 1, 2)
    index = place % SEG

    def bit(number):
        return (index >> number) & 1

    def same(number):
        return bit(number) == (anchor >> number) & 1

    rows = tokens // IN_CHUNKS
    own = []
    for start in range(0, tokens, rows):
        piece = frame[:, start : start + rows]
        if own:
            piece = tied(piece, *own[-1])
        own.append([piece] + [shifted(piece, 0, step) for step in range(1, parts)])

    block = frame
    for number in range(SEG.bit_length() - 1):
        kept = sent = block
        if number < 2:
            half = block.shape[1] // 2
            low, high = block[:, :half], block[:, half:]
            kept = jnp.where(bit(number) == 0, low, high)
            sent = jnp.where(bit(number) == 0, high, low)
        came = exchanged(sent, 1 << number)
        if number == 1:
            w_out = tied(w_out, sent).T
            came = tied(came, w_out)
        block = jnp.where(same(number), kept, came)
    block, own = lax.optimization_barrier((block, own))
    near = [block] + [shifted(block, 0, step) for step in range(1, parts)]
    across = [shifted(block, 2, step) for step in range(parts)]
    queries, *own_kv = project(own, order, modulation, w_qkv, True)
    near = [tied(near[0], queries)] + near[1:]
    near_kv = project([near, across], order, modulation, w_qkv, False)
    kvs = [own_kv, near_kv, [exchanged(x, 1) for x in near_kv]]

    gate = lax.dynamic_slice_in_dim(modulation[2], me * width, width, 0)[:, None]
    rows = tokens // OUT_CHUNKS
    odd = []
    for h in range(parts):
        for f in range(1, count - 1, 2):
            here, there = f * parts + h, (f + 1) * parts + h
            odd += [(here, there), (there, here)]
        for f in (0, count - 1):
            odd.append((f * parts + h, f * parts + (h + 1) % parts))
    is_even = place % 2 == 0
    tap_near = jnp.where(is_even, conv_taps[2], conv_taps[0])
    tap_far = jnp.where(is_even, conv_taps[0], conv_taps[2])
    tap_far = jnp.where((place == 0) | (place == count - 1), 0.0, tap_far)
    taps = jnp.stack([tap_near, conv_taps[1], tap_far]).T
    totals, received = [], []
    for chunk in range(OUT_CHUNKS):
        turn = me_ref
        total, send = attend(turn, parts, queries, kvs, w_out, chunk * rows, rows)
        totals.append(total)
        received.append([shifted(send[step - 1], 0, step) for step in range(1, parts)])
    out, sent = None, []
    for chunk in range(OUT_CHUNKS):
        total = tied(totals[chunk], totals[-1], *sent)
        for part in received[chunk]:
            total = total + part.astype(jnp.float32)
        piece = frame[:, chunk * rows : (chunk + 1) * rows].astype(jnp.float32)
        hidden = (piece + gate * total).astype(jnp.bfloat16)
        sent = [hidden]
        close, far = exchanged(hidden, 1), lax.ppermute(hidden, ("tm", "head"), odd)
        out = convolved(hidden, close, far, taps, chunk * rows, tokens, out)
    return out.T[None]


def solution(mesh):
    in_specs = (
        P("tm", None, "head"),
        P(),
        P(None, None, "head"),
        P("head", None),
        P(None, "head"),
        P(),
    )
    out_specs = P("tm", None, "head")
    return jax.shard_map(local, mesh=mesh, in_specs=in_specs, out_specs=out_specs, check_vma=False)
```

```python
import functools

import jax
import jax.numpy as jnp
from jax import lax
from jax.experimental import pallas as pl
from jax.experimental.pallas import tpu as pltpu
from jax.sharding import PartitionSpec as P

HS = 72
SEG = 16
LANES = 128
VALUE_ROWS = 80
EPSILON = 1e-06
LOG2_E = 1.4426950408889634

CUTS = (0, 2, 4)
CONV_FLOPS = 10**10
VMEM_BYTES = 24 * 2**20
VMEM = pl.BlockSpec(memory_space=pltpu.VMEM)
SMEM = pl.BlockSpec(memory_space=pltpu.SMEM)
HBM = pl.BlockSpec(memory_space=pltpu.HBM)


def outside(x):
    return pltpu.with_memory_space_constraint(x, pltpu.HBM)


def exchanged(block, bit):
    count = lax.axis_size("tm")
    return lax.ppermute(block, "tm", [(i, i ^ bit) for i in range(count)])


def shifted(block, bit, shift):
    frames, heads = lax.axis_size("tm"), lax.axis_size("head")
    route = [
        (f * heads + h, (f ^ bit) * heads + (h + shift) % heads)
        for f in range(frames)
        for h in range(heads)
    ]
    return lax.ppermute(block, ("tm", "head"), route)


def project_kernel(blocks, parts, factor, order_ref, modulation_ref, w_hbm, *refs):
    pieces = refs[: blocks * parts]
    *query_ref, key_ref, value_ref, x_ref, shift_ref, scale_ref, w_ref, w_sem = refs[blocks * parts :]
    features, tokens = x_ref.shape
    width = features // parts
    heads = key_ref.shape[0]
    count = w_ref.shape[0]
    loads = [
        pltpu.make_async_copy(w_hbm.at[3 - count + c], w_ref.at[c], w_sem.at[c]) for c in range(count)
    ]
    for load in loads:
        load.start()
    first = 0
    for block in range(blocks):
        for part, piece in enumerate(pieces[block * parts : (block + 1) * parts]):
            start = pl.multiple_of(order_ref[part] * width, 32)
            x_ref[pl.ds(start, width), first : first + piece.shape[1]] = piece[...]
        first += piece.shape[1]
    columns = as_columns(modulation_ref)
    shift_ref[...] = jnp.broadcast_to(columns[:, 0:1], (features, LANES))
    scale_ref[...] = jnp.broadcast_to(1.0 + columns[:, 1:2], (features, LANES))
    for start in range(0, tokens, LANES):
        values = x_ref[:, start : start + LANES].astype(jnp.float32)
        centred = values - jnp.sum(values, axis=0, keepdims=True) / features
        variance = jnp.sum(centred * centred, axis=0, keepdims=True) / features
        normed = centred * lax.rsqrt(variance + EPSILON)
        x_ref[:, start : start + LANES] = (normed * scale_ref[...] + shift_ref[...]).astype(jnp.bfloat16)

    row = lax.broadcasted_iota(jnp.int32, (VALUE_ROWS - HS, tokens), 0)
    ones = jnp.where(row == 0, 1.0, 0.0).astype(jnp.bfloat16)
    group = 2
    for c in range(count):
        loads[c].wait()
        for first in range(0, heads, group):
            total = jnp.dot(
                w_ref[c, first * HS : (first + group) * HS],
                x_ref[...],
                preferred_element_type=jnp.float32,
            )
            for head in range(first, first + group):
                rows = total[(head - first) * HS : (head - first + 1) * HS]
                if c == count - 1:
                    value_ref[head, 0:HS, :] = rows.astype(jnp.bfloat16)
                    value_ref[head, HS:, :] = ones
                elif c == count - 2:
                    key_ref[head, :, 0:HS] = rows.T.astype(jnp.bfloat16)
                    key_ref[head, :, HS:] = jnp.zeros((tokens, LANES - HS), jnp.bfloat16)
                else:
                    query_ref[0][head, 0:HS, :] = (rows * factor).astype(jnp.bfloat16)
                    query_ref[0][head, HS:, :] = jnp.zeros((LANES - HS, tokens), jnp.bfloat16)


def project(blocks, order, modulation, w_qkv, with_queries):
    parts = len(blocks[0])
    tokens = sum(block[0].shape[1] for block in blocks)
    _, width, features = w_qkv.shape
    heads = width // HS
    count = 3 if with_queries else 2
    queries = jax.ShapeDtypeStruct((heads, LANES, tokens), jnp.bfloat16)
    keys = jax.ShapeDtypeStruct((heads, tokens, LANES), jnp.bfloat16)
    values = jax.ShapeDtypeStruct((heads, VALUE_ROWS, tokens), jnp.bfloat16)
    flat = [piece for block in blocks for piece in block]
    return pl.pallas_call(
        functools.partial(project_kernel, len(blocks), parts, HS ** (-0.5) * LOG2_E),
        out_shape=[queries, keys, values][3 - count :],
        in_specs=[SMEM, VMEM, HBM] + [VMEM] * len(flat),
        out_specs=[VMEM] * count,
        scratch_shapes=[
            pltpu.VMEM((features, tokens), jnp.bfloat16),
            pltpu.VMEM((features, LANES), jnp.float32),
            pltpu.VMEM((features, LANES), jnp.float32),
            pltpu.VMEM((count, width, features), jnp.bfloat16),
            pltpu.SemaphoreType.DMA((count,)),
        ],
        compiler_params=pltpu.CompilerParams(vmem_limit_bytes=VMEM_BYTES),
        cost_estimate=pl.CostEstimate(
            flops=2 * tokens * features * width * count,
            bytes_accessed=count * 2 * (features * width + tokens * heads * LANES),
            transcendentals=0,
        ),
    )(order, modulation, outside(w_qkv), *flat)


def flash(heads, score, weigh, collect):
    for head in range(heads + 2):
        if head < heads:
            score(head)
        if head >= 2:
            collect(head - 2)
        if 1 <= head <= heads:
            weigh(head - 1)


def block_kernel(q_ref, k_ref, v_ref, *refs):
    *before_ref, state_ref, scores, weights, tops = refs
    heads = q_ref.shape[0]

    def score(head):
        scores[head % 2] = jnp.dot(k_ref[head], q_ref[head], preferred_element_type=jnp.float32)

    def weigh(head):
        values = scores[head % 2]
        top = jnp.max(values, axis=0, keepdims=True)
        if before_ref:
            top = jnp.maximum(top, before_ref[0][head, HS + 1 : HS + 2, :])
        tops[head : head + 1, :] = top
        weights[head % 2] = jnp.exp2(values - top).astype(jnp.bfloat16)

    def collect(head):
        total = jnp.dot(v_ref[head], weights[head % 2], preferred_element_type=jnp.float32)
        if before_ref:
            before = before_ref[0][head]
            total += before * jnp.exp2(before[HS + 1 : HS + 2] - tops[head : head + 1, :])
        state_ref[head] = total
        state_ref[head, HS + 1 : HS + 2, :] = tops[head : head + 1, :]

    flash(heads, score, weigh, collect)


def attend_block(queries, keys, values, *state):
    heads, _, tokens = queries.shape
    count = keys.shape[1]
    return pl.pallas_call(
        block_kernel,
        out_shape=jax.ShapeDtypeStruct((heads, VALUE_ROWS, tokens), jnp.float32),
        in_specs=[VMEM] * (3 + len(state)),
        out_specs=VMEM,
        scratch_shapes=[
            pltpu.VMEM((2, count, tokens), jnp.float32),
            pltpu.VMEM((2, count, tokens), jnp.bfloat16),
            pltpu.VMEM((heads, tokens), jnp.float32),
        ],
        compiler_params=pltpu.CompilerParams(vmem_limit_bytes=VMEM_BYTES),
        cost_estimate=pl.CostEstimate(
            flops=4 * heads * tokens * tokens * LANES,
            bytes_accessed=8 * heads * tokens * LANES,
            transcendentals=heads * tokens * tokens,
        ),
    )(queries, keys, values, *state)


def as_columns(rows_ref):
    count, features = rows_ref.shape
    return jnp.concatenate([rows_ref[...], jnp.zeros((8 - count, features), jnp.float32)]).T


def attend_kernel(parts, bounds, blocks, me_ref, modulation_ref, frame_ref, q_ref, state_ref, *refs):
    keys, values = refs[: 2 * blocks : 2], refs[1 : 2 * blocks : 2]
    w_ref = refs[2 * blocks]
    chunks = len(bounds) - 1
    owns, sends = refs[-5 - 2 * chunks : -5 - chunks], refs[-5 - chunks : -5]
    attended, terms, scores, weights, tops = refs[-5:]
    heads = q_ref.shape[0]
    width = frame_ref.shape[0]
    spans, total = [], 0
    for ref in keys:
        spans.append((total, total + ref.shape[1]))
        total += ref.shape[1]

    def score(head):
        for ref, (low, high) in zip(keys, spans):
            scores[head % 2, low:high] = jnp.dot(
                ref[head], q_ref[head], preferred_element_type=jnp.float32
            )

    def weigh(head):
        values = scores[head % 2]
        top = jnp.max(values, axis=0, keepdims=True)
        top = jnp.maximum(top, state_ref[head, HS + 1 : HS + 2, :])
        tops[head : head + 1, :] = top
        weights[head % 2] = jnp.exp2(values - top).astype(jnp.bfloat16)

    def collect(head):
        before = state_ref[head]
        total = before * jnp.exp2(before[HS + 1 : HS + 2] - tops[head : head + 1, :])
        for ref, (low, high) in zip(values, spans):
            total += jnp.dot(
                ref[head], weights[head % 2, low:high], preferred_element_type=jnp.float32
            )
        attended[head * HS : (head + 1) * HS, :] = total[:HS] / total[HS : HS + 1]

    flash(heads, score, weigh, collect)
    gate = as_columns(modulation_ref)[:, 2:3]
    me = me_ref[0]
    terms[...] = gate * jnp.dot(
        w_ref[...], attended[...].astype(jnp.bfloat16), preferred_element_type=jnp.float32
    )
    for start, end, own_ref, send_ref in zip(bounds[:-1], bounds[1:], owns, sends):
        residual = frame_ref[:, start:end].astype(jnp.float32)
        mine = pl.ds(pl.multiple_of(me * width, 32), width)
        own_ref[...] = residual + terms[mine, start:end]
        for step in range(1, parts):
            other = pl.multiple_of(lax.rem(me + step, parts) * width, 32)
            send_ref[step - 1] = terms[pl.ds(other, width), start:end].astype(jnp.bfloat16)


def attend(me, parts, modulation, frame, queries, state, kvs, w_out, bounds):
    heads, _, tokens = queries.shape
    features, width = w_out.shape
    part = features // parts
    keys = sum(k.shape[1] for k, _ in kvs)
    rows = [end - start for start, end in zip(bounds[:-1], bounds[1:])]
    outs = pl.pallas_call(
        functools.partial(attend_kernel, parts, bounds, len(kvs)),
        out_shape=[jax.ShapeDtypeStruct((part, r), jnp.float32) for r in rows]
        + [jax.ShapeDtypeStruct((parts - 1, part, r), jnp.bfloat16) for r in rows],
        in_specs=[SMEM] + [VMEM] * (5 + 2 * len(kvs)),
        out_specs=[VMEM] * (2 * len(rows)),
        scratch_shapes=[
            pltpu.VMEM((heads * HS, tokens), jnp.float32),
            pltpu.VMEM((features, tokens), jnp.float32),
            pltpu.VMEM((2, keys, tokens), jnp.float32),
            pltpu.VMEM((2, keys, tokens), jnp.bfloat16),
            pltpu.VMEM((heads, tokens), jnp.float32),
        ],
        compiler_params=pltpu.CompilerParams(vmem_limit_bytes=VMEM_BYTES),
        cost_estimate=pl.CostEstimate(
            flops=4 * heads * tokens * tokens * LANES + 2 * tokens * w_out.size,
            bytes_accessed=8 * heads * tokens * LANES + 2 * w_out.size,
            transcendentals=heads * tokens * tokens,
        ),
    )(me, modulation, frame, queries, state, *[x for kv in kvs for x in kv], w_out)
    return outs[: len(rows)], outs[len(rows) :]


def conv_kernel(start, taps_ref, hidden_ref, near_ref, far_ref, *refs):
    out_hbm, out_ref, sem = refs[-3:]
    hidden = hidden_ref[...].astype(jnp.float32)
    total = hidden + taps_ref[:, 1:2] * hidden
    total += taps_ref[:, 0:1] * near_ref[...].astype(jnp.float32)
    total += taps_ref[:, 2:3] * far_ref[...].astype(jnp.float32)
    out_ref[...] = total.astype(jnp.bfloat16)
    rows = out_ref.shape[1]
    store = pltpu.make_async_copy(out_ref, out_hbm.at[:, start : start + rows], sem)
    store.start()
    store.wait()


def convolved(taps, hidden, near, far, start, tokens, out):
    width, rows = hidden.shape
    before = [] if out is None else [out]
    return pl.pallas_call(
        functools.partial(conv_kernel, start),
        out_shape=jax.ShapeDtypeStruct((width, tokens), jnp.bfloat16),
        in_specs=[VMEM] * 4 + [HBM] * len(before),
        out_specs=HBM,
        scratch_shapes=[pltpu.VMEM((width, rows), jnp.bfloat16), pltpu.SemaphoreType.DMA],
        input_output_aliases={4: 0} if before else {},
        compiler_params=pltpu.CompilerParams(vmem_limit_bytes=VMEM_BYTES),
        cost_estimate=pl.CostEstimate(
            flops=CONV_FLOPS, bytes_accessed=8 * width * rows, transcendentals=0
        ),
    )(taps, hidden, near, far, *before)


def tied(x, *others):
    return lax.optimization_barrier((x, *others))[0]


def local(frames, modulation, w_qkv, w_out, conv_taps, anchors):
    frame = frames[0].T
    width, tokens = frame.shape
    parts, count = lax.axis_size("head"), lax.axis_size("tm")
    place, me = lax.axis_index("tm"), lax.axis_index("head")
    anchor = lax.dynamic_index_in_dim(anchors, place // SEG, 0, keepdims=False)
    order = ((me - jnp.arange(parts)) % parts).astype(jnp.int32)
    me_ref = me.astype(jnp.int32).reshape(1)
    w_qkv = jnp.swapaxes(w_qkv, 1, 2)
    index = place % SEG

    def bit(number):
        return (index >> number) & 1

    def same(number):
        return bit(number) == (anchor >> number) & 1

    own = [[frame] + [shifted(frame, 0, step) for step in range(1, parts)]]

    def halves(block, number):
        half = block.shape[1] // 2
        low, high = block[:, :half], block[:, half:]
        return jnp.where(bit(number) == 0, low, high), jnp.where(bit(number) == 0, high, low)

    kept, sent = lax.optimization_barrier(halves(frame, 0))
    block = jnp.where(same(0), kept, exchanged(sent, 1))
    kept, sent = halves(block, 1)
    came = lax.cond(anchors[0] >= 0, lambda x: exchanged(x, 2), jnp.zeros_like, sent)
    block = jnp.where(same(1), kept, came)
    for number in range(2, SEG.bit_length() - 1):
        sent = block
        came = exchanged(sent, 1 << number)
        if number == 2:
            w_out = tied(w_out, sent).T
            came = tied(came, w_out)
        if number == 3:
            own[0][0] = tied(own[0][0], sent)
            queries, *own_kv = project(own, order, modulation, w_qkv, True)
            came = tied(came, queries)
        block = jnp.where(same(number), block, came)
    near = [block] + [shifted(block, 0, step) for step in range(1, parts)]
    across = [shifted(block, 2, step) for step in range(parts)]
    state = attend_block(tied(queries, block), *own_kv)
    near[0] = tied(near[0], state)
    near_kv = project([near, across], order, modulation, w_qkv, False)
    far_kv = [exchanged(x, 1) for x in near_kv]
    state = attend_block(queries, *near_kv, state)
    kvs = [[tied(x, state) for x in far_kv]]

    odd = []
    for h in range(parts):
        for f in range(1, count - 1, 2):
            here, there = f * parts + h, (f + 1) * parts + h
            odd += [(here, there), (there, here)]
        for f in (0, count - 1):
            odd.append((f * parts + h, f * parts + (h + 1) % parts))
    is_even = place % 2 == 0
    tap_near = jnp.where(is_even, conv_taps[2], conv_taps[0])
    tap_far = jnp.where(is_even, conv_taps[0], conv_taps[2])
    tap_far = jnp.where((place == 0) | (place == count - 1), 0.0, tap_far)
    taps = jnp.stack([tap_near, conv_taps[1], tap_far]).T
    bounds = [tokens * cut // 4 for cut in CUTS]
    spans = list(zip(bounds[:-1], bounds[1:]))
    totals, sends = attend(me_ref, parts, modulation, frame, queries, state, kvs, w_out, bounds)
    received = [[shifted(send[step - 1], 0, step) for step in range(1, parts)] for send in sends]
    out, sent = None, []
    for chunk, (start, end) in enumerate(spans):
        total = tied(totals[chunk], *sent)
        for part in received[chunk]:
            total = total + part.astype(jnp.float32)
        hidden = total.astype(jnp.bfloat16)
        sent = [hidden]
        close, far = exchanged(hidden, 1), lax.ppermute(hidden, ("tm", "head"), odd)
        out = convolved(taps, hidden, close, far, start, tokens, out)
    return out.T[None]


def solution(mesh):
    in_specs = (
        P("tm", None, "head"),
        P(),
        P(None, None, "head"),
        P("head", None),
        P(None, "head"),
        P(),
    )
    out_specs = P("tm", None, "head")
    return jax.shard_map(local, mesh=mesh, in_specs=in_specs, out_specs=out_specs, check_vma=False)
```

```python
import functools

import jax
import jax.numpy as jnp
from jax import lax
from jax.experimental import pallas as pl
from jax.experimental.pallas import tpu as pltpu
from jax.sharding import PartitionSpec as P

HS = 72
SEG = 16
LANES = 128
VALUE_ROWS = 80
EPSILON = 1e-06
LOG2_E = 1.4426950408889634

CUTS = (0, 2, 4)
CONV_FLOPS = 10**10
VMEM_BYTES = 24 * 2**20
VMEM = pl.BlockSpec(memory_space=pltpu.VMEM)
SMEM = pl.BlockSpec(memory_space=pltpu.SMEM)
HBM = pl.BlockSpec(memory_space=pltpu.HBM)


def outside(x):
    return pltpu.with_memory_space_constraint(x, pltpu.HBM)


def exchanged(block, bit):
    count = lax.axis_size("tm")
    return lax.ppermute(block, "tm", [(i, i ^ bit) for i in range(count)])


def shifted(block, bit, shift):
    frames, heads = lax.axis_size("tm"), lax.axis_size("head")
    route = [
        (f * heads + h, (f ^ bit) * heads + (h + shift) % heads)
        for f in range(frames)
        for h in range(heads)
    ]
    return lax.ppermute(block, ("tm", "head"), route)


def project_kernel(blocks, parts, with_queries, factor, order_ref, modulation_ref, w_hbm, *refs):
    pieces = refs[: blocks * parts]
    *query_ref, key_ref, value_ref, x_ref, shift_ref, scale_ref, w_ref, w_sem = refs[blocks * parts :]
    features, tokens = x_ref.shape
    width = features // parts
    heads = key_ref.shape[0]
    count = w_ref.shape[0]
    loads = []
    if with_queries:
        loads = [
            pltpu.make_async_copy(w_hbm.at[c], w_ref.at[c], w_sem.at[c]) for c in range(count)
        ]
    if with_queries:
        for load in loads:
            load.start()
    first = 0
    for block in range(blocks):
        for part, piece in enumerate(pieces[block * parts : (block + 1) * parts]):
            start = pl.multiple_of(order_ref[part] * width, 32)
            x_ref[pl.ds(start, width), first : first + piece.shape[1]] = piece[...]
        first += piece.shape[1]
    columns = as_columns(modulation_ref)
    shift_ref[...] = jnp.broadcast_to(columns[:, 0:1], (features, LANES))
    scale_ref[...] = jnp.broadcast_to(1.0 + columns[:, 1:2], (features, LANES))
    for start in range(0, tokens, LANES):
        values = x_ref[:, start : start + LANES].astype(jnp.float32)
        centred = values - jnp.sum(values, axis=0, keepdims=True) / features
        variance = jnp.sum(centred * centred, axis=0, keepdims=True) / features
        normed = centred * lax.rsqrt(variance + EPSILON)
        x_ref[:, start : start + LANES] = (normed * scale_ref[...] + shift_ref[...]).astype(jnp.bfloat16)

    row = lax.broadcasted_iota(jnp.int32, (VALUE_ROWS - HS, tokens), 0)
    ones = jnp.where(row == 0, 1.0, 0.0).astype(jnp.bfloat16)
    group = 2
    for c in range(count):
        if with_queries:
            loads[c].wait()
        for first in range(0, heads, group):
            span = slice(first * HS, (first + group) * HS)
            total = jnp.dot(
                w_ref[c, span] if with_queries else w_hbm[c + 1, span],
                x_ref[...],
                preferred_element_type=jnp.float32,
            )
            for head in range(first, first + group):
                rows = total[(head - first) * HS : (head - first + 1) * HS]
                if c == count - 1:
                    value_ref[head, 0:HS, :] = rows.astype(jnp.bfloat16)
                    value_ref[head, HS:, :] = ones
                elif c == count - 2:
                    key_ref[head, :, 0:HS] = rows.T.astype(jnp.bfloat16)
                    key_ref[head, :, HS:] = jnp.zeros((tokens, LANES - HS), jnp.bfloat16)
                else:
                    query_ref[0][head, 0:HS, :] = (rows * factor).astype(jnp.bfloat16)
                    query_ref[0][head, HS:, :] = jnp.zeros((LANES - HS, tokens), jnp.bfloat16)


def project(blocks, order, modulation, w_qkv, with_queries):
    parts = len(blocks[0])
    tokens = sum(block[0].shape[1] for block in blocks)
    _, width, features = w_qkv.shape
    heads = width // HS
    count = 3 if with_queries else 2
    queries = jax.ShapeDtypeStruct((heads, LANES, tokens), jnp.bfloat16)
    keys = jax.ShapeDtypeStruct((heads, tokens, LANES), jnp.bfloat16)
    values = jax.ShapeDtypeStruct((heads, VALUE_ROWS, tokens), jnp.bfloat16)
    flat = [piece for block in blocks for piece in block]
    return pl.pallas_call(
        functools.partial(
            project_kernel, len(blocks), parts, with_queries, HS ** (-0.5) * LOG2_E
        ),
        out_shape=[queries, keys, values][3 - count :],
        in_specs=[SMEM, VMEM, HBM if with_queries else VMEM] + [VMEM] * len(flat),
        out_specs=[VMEM] * count,
        scratch_shapes=[
            pltpu.VMEM((features, tokens), jnp.bfloat16),
            pltpu.VMEM((features, LANES), jnp.float32),
            pltpu.VMEM((features, LANES), jnp.float32),
            pltpu.VMEM((count, width, features), jnp.bfloat16),
            pltpu.SemaphoreType.DMA((count,)),
        ],
        compiler_params=pltpu.CompilerParams(vmem_limit_bytes=VMEM_BYTES),
        cost_estimate=pl.CostEstimate(
            flops=2 * tokens * features * width * count,
            bytes_accessed=count * 2 * (features * width + tokens * heads * LANES),
            transcendentals=0,
        ),
    )(order, modulation, outside(w_qkv) if with_queries else w_qkv, *flat)


def flash(heads, score, weigh, collect):
    for head in range(heads + 2):
        if head < heads:
            score(head)
        if head >= 2:
            collect(head - 2)
        if 1 <= head <= heads:
            weigh(head - 1)


def block_kernel(q_ref, k_ref, v_ref, *refs):
    *before_ref, state_ref, scores, weights, tops = refs
    heads = q_ref.shape[0]

    def score(head):
        scores[head % 2] = jnp.dot(k_ref[head], q_ref[head], preferred_element_type=jnp.float32)

    def weigh(head):
        values = scores[head % 2]
        top = jnp.max(values, axis=0, keepdims=True)
        if before_ref:
            top = jnp.maximum(top, before_ref[0][head, HS + 1 : HS + 2, :])
        tops[head : head + 1, :] = top
        weights[head % 2] = jnp.exp2(values - top).astype(jnp.bfloat16)

    def collect(head):
        total = jnp.dot(v_ref[head], weights[head % 2], preferred_element_type=jnp.float32)
        if before_ref:
            before = before_ref[0][head]
            total += before * jnp.exp2(before[HS + 1 : HS + 2] - tops[head : head + 1, :])
        state_ref[head] = total
        state_ref[head, HS + 1 : HS + 2, :] = tops[head : head + 1, :]

    flash(heads, score, weigh, collect)


def attend_block(queries, keys, values, *state):
    heads, _, tokens = queries.shape
    count = keys.shape[1]
    return pl.pallas_call(
        block_kernel,
        out_shape=jax.ShapeDtypeStruct((heads, VALUE_ROWS, tokens), jnp.float32),
        in_specs=[VMEM] * (3 + len(state)),
        out_specs=VMEM,
        scratch_shapes=[
            pltpu.VMEM((2, count, tokens), jnp.float32),
            pltpu.VMEM((2, count, tokens), jnp.bfloat16),
            pltpu.VMEM((heads, tokens), jnp.float32),
        ],
        compiler_params=pltpu.CompilerParams(vmem_limit_bytes=VMEM_BYTES),
        cost_estimate=pl.CostEstimate(
            flops=4 * heads * tokens * tokens * LANES,
            bytes_accessed=8 * heads * tokens * LANES,
            transcendentals=heads * tokens * tokens,
        ),
    )(queries, keys, values, *state)


def as_columns(rows_ref):
    count, features = rows_ref.shape
    return jnp.concatenate([rows_ref[...], jnp.zeros((8 - count, features), jnp.float32)]).T


def attend_kernel(parts, bounds, blocks, me_ref, modulation_ref, frame_ref, q_ref, state_ref, *refs):
    keys, values = refs[: 2 * blocks : 2], refs[1 : 2 * blocks : 2]
    w_ref = refs[2 * blocks]
    chunks = len(bounds) - 1
    owns, sends = refs[-7 - 2 * chunks : -7 - chunks], refs[-7 - chunks : -7]
    attended, terms, scores, weights, tops, held, sem = refs[-7:]
    heads = q_ref.shape[0]
    width = frame_ref.shape[0]
    spans, total = [], 0
    for ref in keys:
        spans.append((total, total + ref.shape[1]))
        total += ref.shape[1]

    def score(head):
        for ref, (low, high) in zip(keys, spans):
            scores[head % 2, low:high] = jnp.dot(
                ref[head], q_ref[head], preferred_element_type=jnp.float32
            )

    def weigh(head):
        values = scores[head % 2]
        top = jnp.max(values, axis=0, keepdims=True)
        top = jnp.maximum(top, state_ref[head, HS + 1 : HS + 2, :])
        tops[head : head + 1, :] = top
        weights[head % 2] = jnp.exp2(values - top).astype(jnp.bfloat16)

    def collect(head):
        before = state_ref[head]
        total = before * jnp.exp2(before[HS + 1 : HS + 2] - tops[head : head + 1, :])
        for ref, (low, high) in zip(values, spans):
            total += jnp.dot(
                ref[head], weights[head % 2, low:high], preferred_element_type=jnp.float32
            )
        attended[head * HS : (head + 1) * HS, :] = total[:HS] / total[HS : HS + 1]

    flash(heads, score, weigh, collect)
    gate = as_columns(modulation_ref)[:, 2:3]
    me = me_ref[0]
    terms[...] = gate * jnp.dot(
        w_ref[...], attended[...].astype(jnp.bfloat16), preferred_element_type=jnp.float32
    )
    mine = pl.ds(pl.multiple_of(me * width, 32), width)
    held[...] = frame_ref[:, bounds[-2] :].astype(jnp.float32) + terms[mine, bounds[-2] :]
    store = pltpu.make_async_copy(held, owns[-1], sem)
    store.start()
    for start, end, own_ref, send_ref in zip(bounds[:-1], bounds[1:], owns, sends):
        if end < bounds[-1]:
            residual = frame_ref[:, start:end].astype(jnp.float32)
            own_ref[...] = residual + terms[mine, start:end]
        for step in range(1, parts):
            other = pl.multiple_of(lax.rem(me + step, parts) * width, 32)
            send_ref[step - 1] = terms[pl.ds(other, width), start:end].astype(jnp.bfloat16)
    store.wait()


def attend(me, parts, modulation, frame, queries, state, kvs, w_out, bounds):
    heads, _, tokens = queries.shape
    features, width = w_out.shape
    part = features // parts
    keys = sum(k.shape[1] for k, _ in kvs)
    rows = [end - start for start, end in zip(bounds[:-1], bounds[1:])]
    outs = pl.pallas_call(
        functools.partial(attend_kernel, parts, bounds, len(kvs)),
        out_shape=[jax.ShapeDtypeStruct((part, r), jnp.float32) for r in rows[:-1]]
        + [pltpu.HBM((part, rows[-1]), jnp.float32)]
        + [jax.ShapeDtypeStruct((parts - 1, part, r), jnp.bfloat16) for r in rows],
        in_specs=[SMEM] + [VMEM] * (5 + 2 * len(kvs)),
        out_specs=[VMEM] * (len(rows) - 1) + [HBM] + [VMEM] * len(rows),
        scratch_shapes=[
            pltpu.VMEM((heads * HS, tokens), jnp.float32),
            pltpu.VMEM((features, tokens), jnp.float32),
            pltpu.VMEM((2, keys, tokens), jnp.float32),
            pltpu.VMEM((2, keys, tokens), jnp.bfloat16),
            pltpu.VMEM((heads, tokens), jnp.float32),
            pltpu.VMEM((part, rows[-1]), jnp.float32),
            pltpu.SemaphoreType.DMA,
        ],
        compiler_params=pltpu.CompilerParams(vmem_limit_bytes=VMEM_BYTES),
        cost_estimate=pl.CostEstimate(
            flops=4 * heads * tokens * tokens * LANES + 2 * tokens * w_out.size,
            bytes_accessed=8 * heads * tokens * LANES + 2 * w_out.size,
            transcendentals=heads * tokens * tokens,
        ),
    )(me, modulation, frame, queries, state, *[x for kv in kvs for x in kv], w_out)
    return outs[: len(rows)], outs[len(rows) :]


def conv_kernel(start, taps_ref, hidden_ref, near_ref, far_ref, *refs):
    out_hbm, out_ref, sem = refs[-3:]
    hidden = hidden_ref[...].astype(jnp.float32)
    total = hidden + taps_ref[:, 1:2] * hidden
    total += taps_ref[:, 0:1] * near_ref[...].astype(jnp.float32)
    total += taps_ref[:, 2:3] * far_ref[...].astype(jnp.float32)
    out_ref[...] = total.astype(jnp.bfloat16)
    rows = out_ref.shape[1]
    store = pltpu.make_async_copy(out_ref, out_hbm.at[:, start : start + rows], sem)
    store.start()
    store.wait()


def convolved(taps, hidden, near, far, start, tokens, out):
    width, rows = hidden.shape
    before = [] if out is None else [out]
    return pl.pallas_call(
        functools.partial(conv_kernel, start),
        out_shape=jax.ShapeDtypeStruct((width, tokens), jnp.bfloat16),
        in_specs=[VMEM] * 4 + [HBM] * len(before),
        out_specs=HBM,
        scratch_shapes=[pltpu.VMEM((width, rows), jnp.bfloat16), pltpu.SemaphoreType.DMA],
        input_output_aliases={4: 0} if before else {},
        compiler_params=pltpu.CompilerParams(vmem_limit_bytes=VMEM_BYTES),
        cost_estimate=pl.CostEstimate(
            flops=CONV_FLOPS, bytes_accessed=8 * width * rows, transcendentals=0
        ),
    )(taps, hidden, near, far, *before)


def tied(x, *others):
    return lax.optimization_barrier((x, *others))[0]


def local(frames, modulation, w_qkv, w_out, conv_taps, anchors):
    frame = frames[0].T
    width, tokens = frame.shape
    parts, count = lax.axis_size("head"), lax.axis_size("tm")
    place, me = lax.axis_index("tm"), lax.axis_index("head")
    anchor = lax.dynamic_index_in_dim(anchors, place // SEG, 0, keepdims=False)
    order = ((me - jnp.arange(parts)) % parts).astype(jnp.int32)
    me_ref = me.astype(jnp.int32).reshape(1)
    w_qkv = jnp.swapaxes(w_qkv, 1, 2)
    index = place % SEG

    def bit(number):
        return (index >> number) & 1

    def same(number):
        return bit(number) == (anchor >> number) & 1

    own = [[frame] + [shifted(frame, 0, step) for step in range(1, parts)]]

    def halves(block, number):
        half = block.shape[1] // 2
        low, high = block[:, :half], block[:, half:]
        return jnp.where(bit(number) == 0, low, high), jnp.where(bit(number) == 0, high, low)

    kept, sent = lax.optimization_barrier(halves(frame, 0))
    block = jnp.where(same(0), kept, exchanged(sent, 1))
    kept, sent = halves(block, 1)
    came = lax.cond(anchors[0] >= 0, lambda x: exchanged(x, 2), jnp.zeros_like, sent)
    block = jnp.where(same(1), kept, came)
    for number in range(2, SEG.bit_length() - 1):
        sent = block
        came = exchanged(sent, 1 << number)
        if number == 2:
            w_out = tied(w_out, sent).T
            came = tied(came, w_out)
        if number == 3:
            own[0][0] = tied(own[0][0], sent)
            queries, *own_kv = project(own, order, modulation, w_qkv, True)
            came = tied(came, queries)
        block = jnp.where(same(number), block, came)
    near = [block] + [shifted(block, 0, step) for step in range(1, parts)]
    across = [shifted(block, 2, step) for step in range(parts)]
    state = attend_block(tied(queries, block), *own_kv)
    near[0] = tied(near[0], state)
    near_kv = project([near, across], order, modulation, w_qkv, False)
    far_kv = [exchanged(x, 1) for x in near_kv]
    state = attend_block(queries, *near_kv, state)
    kvs = [[tied(x, state) for x in far_kv]]

    odd = []
    for h in range(parts):
        for f in range(1, count - 1, 2):
            here, there = f * parts + h, (f + 1) * parts + h
            odd += [(here, there), (there, here)]
        for f in (0, count - 1):
            odd.append((f * parts + h, f * parts + (h + 1) % parts))
    is_even = place % 2 == 0
    tap_near = jnp.where(is_even, conv_taps[2], conv_taps[0])
    tap_far = jnp.where(is_even, conv_taps[0], conv_taps[2])
    tap_far = jnp.where((place == 0) | (place == count - 1), 0.0, tap_far)
    taps = jnp.stack([tap_near, conv_taps[1], tap_far]).T
    bounds = [tokens * cut // 4 for cut in CUTS]
    spans = list(zip(bounds[:-1], bounds[1:]))
    totals, sends = attend(me_ref, parts, modulation, frame, queries, state, kvs, w_out, bounds)
    received = [[shifted(send[step - 1], 0, step) for step in range(1, parts)] for send in sends]
    out, sent = None, []
    for chunk, (start, end) in enumerate(spans):
        total = tied(totals[chunk], *sent)
        for part in received[chunk]:
            total = total + part.astype(jnp.float32)
        hidden = total.astype(jnp.bfloat16)
        sent = [hidden]
        close, far = exchanged(hidden, 1), lax.ppermute(hidden, ("tm", "head"), odd)
        out = convolved(taps, hidden, close, far, start, tokens, out)
    return out.T[None]


def solution(mesh):
    in_specs = (
        P("tm", None, "head"),
        P(),
        P(None, None, "head"),
        P("head", None),
        P(None, "head"),
        P(),
    )
    out_specs = P("tm", None, "head")
    return jax.shard_map(local, mesh=mesh, in_specs=in_specs, out_specs=out_specs, check_vma=False)
```

```python
import functools

import jax
import jax.numpy as jnp
from jax import lax
from jax.experimental import pallas as pl
from jax.experimental.pallas import tpu as pltpu
from jax.sharding import PartitionSpec as P

HS = 72
SEG = 16
LANES = 128
VALUE_ROWS = 80
EPSILON = 1e-06
LOG2_E = 1.4426950408889634

CUTS = (0, 2, 4)
CONV_FLOPS = 10**10
VMEM_BYTES = 24 * 2**20
VMEM = pl.BlockSpec(memory_space=pltpu.VMEM)
SMEM = pl.BlockSpec(memory_space=pltpu.SMEM)
HBM = pl.BlockSpec(memory_space=pltpu.HBM)


def outside(x):
    return pltpu.with_memory_space_constraint(x, pltpu.HBM)


def exchanged(block, bit):
    count = lax.axis_size("tm")
    return lax.ppermute(block, "tm", [(i, i ^ bit) for i in range(count)])


def shifted(block, bit, shift):
    frames, heads = lax.axis_size("tm"), lax.axis_size("head")
    route = [
        (f * heads + h, (f ^ bit) * heads + (h + shift) % heads)
        for f in range(frames)
        for h in range(heads)
    ]
    return lax.ppermute(block, ("tm", "head"), route)


def project_kernel(blocks, parts, with_queries, factor, order_ref, modulation_ref, w_hbm, *refs):
    pieces = refs[: blocks * parts]
    *query_ref, key_ref, value_ref, x_ref, shift_ref, scale_ref, w_ref, w_sem = refs[blocks * parts :]
    features, tokens = x_ref.shape
    width = features // parts
    heads = key_ref.shape[0]
    count = w_ref.shape[0]
    loads = []
    if with_queries:
        loads = [
            pltpu.make_async_copy(w_hbm.at[c], w_ref.at[c], w_sem.at[c]) for c in range(count)
        ]
    if with_queries:
        for load in loads:
            load.start()
    first = 0
    for block in range(blocks):
        for part, piece in enumerate(pieces[block * parts : (block + 1) * parts]):
            start = pl.multiple_of(order_ref[part] * width, 32)
            x_ref[pl.ds(start, width), first : first + piece.shape[1]] = piece[...]
        first += piece.shape[1]
    columns = as_columns(modulation_ref)
    shift_ref[...] = jnp.broadcast_to(columns[:, 0:1], (features, LANES))
    scale_ref[...] = jnp.broadcast_to(1.0 + columns[:, 1:2], (features, LANES))
    for start in range(0, tokens, LANES):
        values = x_ref[:, start : start + LANES].astype(jnp.float32)
        centred = values - jnp.sum(values, axis=0, keepdims=True) / features
        variance = jnp.sum(centred * centred, axis=0, keepdims=True) / features
        normed = centred * lax.rsqrt(variance + EPSILON)
        x_ref[:, start : start + LANES] = (normed * scale_ref[...] + shift_ref[...]).astype(jnp.bfloat16)

    row = lax.broadcasted_iota(jnp.int32, (VALUE_ROWS - HS, tokens), 0)
    ones = jnp.where(row == 0, 1.0, 0.0).astype(jnp.bfloat16)
    group = 2
    for c in range(count):
        if with_queries:
            loads[c].wait()
        for first in range(0, heads, group):
            span = slice(first * HS, (first + group) * HS)
            total = jnp.dot(
                w_ref[c, span] if with_queries else w_hbm[c + 1, span],
                x_ref[...],
                preferred_element_type=jnp.float32,
            )
            for head in range(first, first + group):
                rows = total[(head - first) * HS : (head - first + 1) * HS]
                if c == count - 1:
                    value_ref[head, 0:HS, :] = rows.astype(jnp.bfloat16)
                    value_ref[head, HS:, :] = ones
                elif c == count - 2:
                    key_ref[head, :, 0:HS] = rows.T.astype(jnp.bfloat16)
                    key_ref[head, :, HS:] = jnp.zeros((tokens, LANES - HS), jnp.bfloat16)
                else:
                    query_ref[0][head, 0:HS, :] = (rows * factor).astype(jnp.bfloat16)
                    query_ref[0][head, HS:, :] = jnp.zeros((LANES - HS, tokens), jnp.bfloat16)


def project(blocks, order, modulation, w_qkv, with_queries):
    parts = len(blocks[0])
    tokens = sum(block[0].shape[1] for block in blocks)
    _, width, features = w_qkv.shape
    heads = width // HS
    count = 3 if with_queries else 2
    queries = jax.ShapeDtypeStruct((heads, LANES, tokens), jnp.bfloat16)
    keys = jax.ShapeDtypeStruct((heads, tokens, LANES), jnp.bfloat16)
    values = jax.ShapeDtypeStruct((heads, VALUE_ROWS, tokens), jnp.bfloat16)
    flat = [piece for block in blocks for piece in block]
    return pl.pallas_call(
        functools.partial(
            project_kernel, len(blocks), parts, with_queries, HS ** (-0.5) * LOG2_E
        ),
        out_shape=[queries, keys, values][3 - count :],
        in_specs=[SMEM, VMEM, HBM if with_queries else VMEM] + [VMEM] * len(flat),
        out_specs=[VMEM] * count,
        scratch_shapes=[
            pltpu.VMEM((features, tokens), jnp.bfloat16),
            pltpu.VMEM((features, LANES), jnp.float32),
            pltpu.VMEM((features, LANES), jnp.float32),
            pltpu.VMEM((count, width, features), jnp.bfloat16),
            pltpu.SemaphoreType.DMA((count,)),
        ],
        compiler_params=pltpu.CompilerParams(vmem_limit_bytes=VMEM_BYTES),
        cost_estimate=pl.CostEstimate(
            flops=2 * tokens * features * width * count,
            bytes_accessed=count * 2 * (features * width + tokens * heads * LANES),
            transcendentals=0,
        ),
    )(order, modulation, outside(w_qkv) if with_queries else w_qkv, *flat)


def flash(heads, score, weigh, collect):
    for head in range(heads + 2):
        if head < heads:
            score(head)
        if head >= 2:
            collect(head - 2)
        if 1 <= head <= heads:
            weigh(head - 1)


def block_kernel(q_ref, k_ref, v_ref, *refs):
    *before_ref, state_ref, scores, weights, tops = refs
    heads = q_ref.shape[0]

    def score(head):
        scores[head % 2] = jnp.dot(k_ref[head], q_ref[head], preferred_element_type=jnp.float32)

    def weigh(head):
        values = scores[head % 2]
        top = jnp.max(values, axis=0, keepdims=True)
        if before_ref:
            top = jnp.maximum(top, before_ref[0][head, HS + 1 : HS + 2, :])
        tops[head : head + 1, :] = top
        weights[head % 2] = jnp.exp2(values - top).astype(jnp.bfloat16)

    def collect(head):
        total = jnp.dot(v_ref[head], weights[head % 2], preferred_element_type=jnp.float32)
        if before_ref:
            before = before_ref[0][head]
            total += before * jnp.exp2(before[HS + 1 : HS + 2] - tops[head : head + 1, :])
        state_ref[head] = total
        state_ref[head, HS + 1 : HS + 2, :] = tops[head : head + 1, :]

    flash(heads, score, weigh, collect)


def attend_block(queries, keys, values, *state):
    heads, _, tokens = queries.shape
    count = keys.shape[1]
    return pl.pallas_call(
        block_kernel,
        out_shape=jax.ShapeDtypeStruct((heads, VALUE_ROWS, tokens), jnp.float32),
        in_specs=[VMEM] * (3 + len(state)),
        out_specs=VMEM,
        scratch_shapes=[
            pltpu.VMEM((2, count, tokens), jnp.float32),
            pltpu.VMEM((2, count, tokens), jnp.bfloat16),
            pltpu.VMEM((heads, tokens), jnp.float32),
        ],
        compiler_params=pltpu.CompilerParams(vmem_limit_bytes=VMEM_BYTES),
        cost_estimate=pl.CostEstimate(
            flops=4 * heads * tokens * tokens * LANES,
            bytes_accessed=8 * heads * tokens * LANES,
            transcendentals=heads * tokens * tokens,
        ),
    )(queries, keys, values, *state)


def as_columns(rows_ref):
    count, features = rows_ref.shape
    return jnp.concatenate([rows_ref[...], jnp.zeros((8 - count, features), jnp.float32)]).T


def attend_kernel(parts, bounds, blocks, me_ref, modulation_ref, frame_ref, q_ref, state_ref, *refs):
    keys, values = refs[: 2 * blocks : 2], refs[1 : 2 * blocks : 2]
    w_ref = refs[2 * blocks]
    chunks = len(bounds) - 1
    owns, sends = refs[-7 - 2 * chunks : -7 - chunks], refs[-7 - chunks : -7]
    attended, terms, scores, weights, tops, held, sem = refs[-7:]
    heads = q_ref.shape[0]
    width = frame_ref.shape[0]
    spans, total = [], 0
    for ref in keys:
        spans.append((total, total + ref.shape[1]))
        total += ref.shape[1]

    def score(head):
        for ref, (low, high) in zip(keys, spans):
            scores[head % 2, low:high] = jnp.dot(
                ref[head], q_ref[head], preferred_element_type=jnp.float32
            )

    def weigh(head):
        values = scores[head % 2]
        top = jnp.max(values, axis=0, keepdims=True)
        top = jnp.maximum(top, state_ref[head, HS + 1 : HS + 2, :])
        tops[head : head + 1, :] = top
        weights[head % 2] = jnp.exp2(values - top).astype(jnp.bfloat16)

    def collect(head):
        before = state_ref[head]
        total = before * jnp.exp2(before[HS + 1 : HS + 2] - tops[head : head + 1, :])
        for ref, (low, high) in zip(values, spans):
            total += jnp.dot(
                ref[head], weights[head % 2, low:high], preferred_element_type=jnp.float32
            )
        attended[head * HS : (head + 1) * HS, :] = total[:HS] / total[HS : HS + 1]

    gate = as_columns(modulation_ref)[:, 2:3]
    flash(heads, score, weigh, collect)
    me = me_ref[0]
    terms[...] = gate * jnp.dot(
        w_ref[...], attended[...].astype(jnp.bfloat16), preferred_element_type=jnp.float32
    )
    mine = pl.ds(pl.multiple_of(me * width, 32), width)
    held[...] = frame_ref[:, bounds[-2] :].astype(jnp.float32) + terms[mine, bounds[-2] :]
    store = pltpu.make_async_copy(held, owns[-1], sem)
    store.start()
    for start, end, own_ref, send_ref in zip(bounds[:-1], bounds[1:], owns, sends):
        if end < bounds[-1]:
            residual = frame_ref[:, start:end].astype(jnp.float32)
            own_ref[...] = residual + terms[mine, start:end]
        for step in range(1, parts):
            other = pl.multiple_of(lax.rem(me + step, parts) * width, 32)
            send_ref[step - 1] = terms[pl.ds(other, width), start:end].astype(jnp.bfloat16)
    store.wait()


def attend(me, parts, modulation, frame, queries, state, kvs, w_out, bounds):
    heads, _, tokens = queries.shape
    features, width = w_out.shape
    part = features // parts
    keys = sum(k.shape[1] for k, _ in kvs)
    rows = [end - start for start, end in zip(bounds[:-1], bounds[1:])]
    outs = pl.pallas_call(
        functools.partial(attend_kernel, parts, bounds, len(kvs)),
        out_shape=[jax.ShapeDtypeStruct((part, r), jnp.float32) for r in rows[:-1]]
        + [pltpu.HBM((part, rows[-1]), jnp.float32)]
        + [jax.ShapeDtypeStruct((parts - 1, part, r), jnp.bfloat16) for r in rows],
        in_specs=[SMEM] + [VMEM] * (5 + 2 * len(kvs)),
        out_specs=[VMEM] * (len(rows) - 1) + [HBM] + [VMEM] * len(rows),
        scratch_shapes=[
            pltpu.VMEM((heads * HS, tokens), jnp.float32),
            pltpu.VMEM((features, tokens), jnp.float32),
            pltpu.VMEM((2, keys, tokens), jnp.float32),
            pltpu.VMEM((2, keys, tokens), jnp.bfloat16),
            pltpu.VMEM((heads, tokens), jnp.float32),
            pltpu.VMEM((part, rows[-1]), jnp.float32),
            pltpu.SemaphoreType.DMA,
        ],
        compiler_params=pltpu.CompilerParams(vmem_limit_bytes=VMEM_BYTES),
        cost_estimate=pl.CostEstimate(
            flops=4 * heads * tokens * tokens * LANES + 2 * tokens * w_out.size,
            bytes_accessed=8 * heads * tokens * LANES + 2 * w_out.size,
            transcendentals=heads * tokens * tokens,
        ),
    )(me, modulation, frame, queries, state, *[x for kv in kvs for x in kv], w_out)
    return outs[: len(rows)], outs[len(rows) :]


def conv_kernel(start, taps_ref, hidden_ref, near_ref, far_ref, *refs):
    out_hbm, out_ref, sem = refs[-3:]
    hidden = hidden_ref[...].astype(jnp.float32)
    total = hidden + taps_ref[:, 1:2] * hidden
    total += taps_ref[:, 0:1] * near_ref[...].astype(jnp.float32)
    total += taps_ref[:, 2:3] * far_ref[...].astype(jnp.float32)
    out_ref[...] = total.astype(jnp.bfloat16)
    rows = out_ref.shape[1]
    store = pltpu.make_async_copy(out_ref, out_hbm.at[:, start : start + rows], sem)
    store.start()
    store.wait()


def convolved(taps, hidden, near, far, start, tokens, out):
    width, rows = hidden.shape
    before = [] if out is None else [out]
    return pl.pallas_call(
        functools.partial(conv_kernel, start),
        out_shape=jax.ShapeDtypeStruct((width, tokens), jnp.bfloat16),
        in_specs=[VMEM] * 4 + [HBM] * len(before),
        out_specs=HBM,
        scratch_shapes=[pltpu.VMEM((width, rows), jnp.bfloat16), pltpu.SemaphoreType.DMA],
        input_output_aliases={4: 0} if before else {},
        compiler_params=pltpu.CompilerParams(vmem_limit_bytes=VMEM_BYTES),
        cost_estimate=pl.CostEstimate(
            flops=CONV_FLOPS, bytes_accessed=8 * width * rows, transcendentals=0
        ),
    )(taps, hidden, near, far, *before)


def tied(x, *others):
    return lax.optimization_barrier((x, *others))[0]


def local(frames, modulation, w_qkv, w_out, conv_taps, anchors):
    frame = frames[0].T
    width, tokens = frame.shape
    parts, count = lax.axis_size("head"), lax.axis_size("tm")
    place, me = lax.axis_index("tm"), lax.axis_index("head")
    anchor = lax.dynamic_index_in_dim(anchors, place // SEG, 0, keepdims=False)
    order = ((me - jnp.arange(parts)) % parts).astype(jnp.int32)
    me_ref = me.astype(jnp.int32).reshape(1)
    w_qkv = jnp.swapaxes(w_qkv, 1, 2)
    index = place % SEG

    def bit(number):
        return (index >> number) & 1

    def same(number):
        return bit(number) == (anchor >> number) & 1

    own = [[frame] + [shifted(frame, 0, step) for step in range(1, parts)]]

    def halves(block, number):
        half = block.shape[1] // 2
        low, high = block[:, :half], block[:, half:]
        return jnp.where(bit(number) == 0, low, high), jnp.where(bit(number) == 0, high, low)

    kept, sent = lax.optimization_barrier(halves(frame, 0))
    block = jnp.where(same(0), kept, exchanged(sent, 1))
    kept, sent = halves(block, 1)
    came = lax.cond(anchors[0] >= 0, lambda x: exchanged(x, 2), jnp.zeros_like, sent)
    block = jnp.where(same(1), kept, came)
    for number in range(2, SEG.bit_length() - 1):
        sent = block
        came = exchanged(sent, 1 << number)
        if number == 2:
            w_out = tied(w_out, sent).T
            came = tied(came, w_out)
        if number == 3:
            own[0][0] = tied(own[0][0], sent)
            queries, *own_kv = project(own, order, modulation, w_qkv, True)
            came = tied(came, queries)
        block = jnp.where(same(number), block, came)
    near = [block] + [shifted(block, 0, step) for step in range(1, parts)]
    across = [shifted(block, 2, step) for step in range(parts)]
    state = attend_block(tied(queries, block), *own_kv)
    near[0] = tied(near[0], state)
    near_kv = project([near, across], order, modulation, w_qkv, False)
    far_kv = [exchanged(x, 1) for x in near_kv]
    state = attend_block(queries, *near_kv, state)
    kvs = [[tied(x, state) for x in far_kv]]

    odd = []
    for h in range(parts):
        for f in range(1, count - 1, 2):
            here, there = f * parts + h, (f + 1) * parts + h
            odd += [(here, there), (there, here)]
        for f in (0, count - 1):
            odd.append((f * parts + h, f * parts + (h + 1) % parts))
    is_even = place % 2 == 0
    tap_near = jnp.where(is_even, conv_taps[2], conv_taps[0])
    tap_far = jnp.where(is_even, conv_taps[0], conv_taps[2])
    tap_far = jnp.where((place == 0) | (place == count - 1), 0.0, tap_far)
    taps = jnp.stack([tap_near, conv_taps[1], tap_far]).T
    bounds = [tokens * cut // 4 for cut in CUTS]
    spans = list(zip(bounds[:-1], bounds[1:]))
    totals, sends = attend(me_ref, parts, modulation, frame, queries, state, kvs, w_out, bounds)
    received = [[shifted(send[step - 1], 0, step) for step in range(1, parts)] for send in sends]
    out, sent = None, []
    for chunk, (start, end) in enumerate(spans):
        total = tied(totals[chunk], *sent)
        for part in received[chunk]:
            total = total + part.astype(jnp.float32)
        hidden = total.astype(jnp.bfloat16)
        sent = [hidden]
        close, far = exchanged(hidden, 1), lax.ppermute(hidden, ("tm", "head"), odd)
        out = convolved(taps, hidden, close, far, start, tokens, out)
    return out.T[None]


def solution(mesh):
    in_specs = (
        P("tm", None, "head"),
        P(),
        P(None, None, "head"),
        P("head", None),
        P(None, "head"),
        P(),
    )
    out_specs = P("tm", None, "head")
    return jax.shard_map(local, mesh=mesh, in_specs=in_specs, out_specs=out_specs, check_vma=False)
```
